256 devices in a mesh: rep: 16 (over z, y_lo), fsdp: 16 (over y_hi, x, core).
Axes of the slice: x: 4, y: 4 (y_hi: 2, y_lo: 2; y = y_hi * 2 + y_lo), z: 8, core: 2. Of those that a mesh axis runs over, the one named last changes fastest.
Arguments:
- param: float32 [16, 512, 8192], P('rep', 'fsdp'), may hold values from -6 to 6
- first: float32 [16, 512, 8192], P('rep', 'fsdp'), may hold values from -6 to 6
- second: float32 [16, 512, 8192], P('rep', 'fsdp'), may hold values from 0.5 to 4
- push_weight: float32 [16], P('rep'), may hold values from 0.5 to 2
- acts: bfloat16 [16, 6144, 8192], P('rep', 'fsdp'), may hold values from -6 to 6
- cotangent: bfloat16 [16, 6144, 512], P('rep', 'fsdp'), may hold values from -0.078125 to 0.078125
- exponent: int32 [1], replicated, may hold values from 0 to 3
Outputs:
- mixed_param: float32 [16, 512, 8192], P('rep', 'fsdp')
- new_first: float32 [16, 512, 8192], P('rep', 'fsdp')
- new_second: float32 [16, 512, 8192], P('rep', 'fsdp')
- mixed_weight: float32 [16], P('rep')
The draws below stay inside these ranges and needn't reach their ends.
All inputs are finite; a program needn't handle non-finite values.
Results may differ from the reference program's by a relative error of at most 0.0003.
Values sent between devices are 32-bit elements; how exact they have to be, the bound alone decides.
No kernel may reach another device: no remote copies, remote signals or barrier semaphores. Data moves between devices by JAX's collectives and lax.ppermute only.
A program may use at most 128 MiB of HBM per device.

```python
import math
import jax
import jax.numpy as jnp
from jax import lax

D = 8192
K_RANGE = 4
TOK_DEV = 384
ROWS = 512
TOKENS = 6144
REPLICAS = 16
N_FSDP = 16


def block_scale(own_key, extent, shards, low, top_value):
    factor_of, own = 1.0, jax.random.fold_in(own_key, 6)
    for axis_at, shards_of in shards:
        steps = jnp.exp(jax.random.uniform(jax.random.fold_in(own, axis_at), (shards_of,), jnp.float32, low / len(shards), top_value / len(shards)))
        factor_of = factor_of * jnp.repeat(steps, extent[axis_at] // shards_of).reshape([-1 if axis == axis_at else 1 for axis in range(len(extent))])
    return factor_of


def noise(own_key, shape, spread, reach, shards=(), kind=jnp.bfloat16):
    level = block_scale(own_key, shape, shards, -0.22, 0.18) if shards else 1.0
    entries = jax.random.normal(own_key, shape, jnp.float32) * spread * level
    return jnp.minimum(jnp.maximum(entries, -reach), reach).astype(kind)


def setup_inputs(seed: int = 0) -> dict:
    arg_keys = jax.random.split(jax.random.key(seed), 8)
    return {
        "param": noise(arg_keys[0], (REPLICAS, ROWS, D), 1.0, 6.0, ((0, 16), (1, 16)), jnp.float32),
        "first": noise(arg_keys[1], (REPLICAS, ROWS, D), 1.0, 6.0, ((0, 16), (1, 16)), jnp.float32),
        "second": jnp.clip(jnp.exp(math.log(4.0) - 2.0794415 * jax.random.uniform(arg_keys[2], (REPLICAS, ROWS, D), jnp.float32) ** block_scale(arg_keys[2], (REPLICAS, ROWS, D), ((0, 16), (1, 16)), -0.2, 0.2)), 0.5, 4.0),
        "push_weight": jnp.clip(jnp.exp(math.log(2.0) - 1.3862944 * jax.random.uniform(arg_keys[3], (REPLICAS,), jnp.float32) ** block_scale(arg_keys[3], (REPLICAS,), ((0, 16),), -0.2, 0.2)), 0.5, 2.0),
        "acts": noise(arg_keys[4], (REPLICAS, TOKENS, D), 1.0, 6.0, ((0, 16), (1, 16))),
        "cotangent": noise(arg_keys[5], (REPLICAS, TOKENS, ROWS), TOKENS ** -0.5, 0.078125, ((0, 16), (1, 16))),
        "exponent": jax.random.randint(arg_keys[6], (1,), 0, K_RANGE).astype(jnp.int32),
    }


def replica_grad(operands):
    acts_rep, cot_rep = operands
    acts_blocks = acts_rep.reshape(N_FSDP, TOK_DEV, D)
    cot_blocks = cot_rep.reshape(N_FSDP, TOK_DEV, ROWS)

    def add_block(total, block):
        act_block, cot_block = block
        partial_term = lax.dot_general(cot_block, act_block, (((0,), (0,)), ((), ())), preferred_element_type=jnp.float32)
        return (total + partial_term, None)
    total, unused = lax.scan(add_block, jnp.zeros((ROWS, D), jnp.float32), (acts_blocks, cot_blocks))
    return total

def reference(param, first, second, push_weight, acts, cotangent, exponent):
    grad = lax.map(replica_grad, (acts, cotangent))
    new_first = 0.9 * first + 0.1 * grad
    new_second = 0.999 * second + 0.001 * grad * grad
    stepped = param - 0.1 * new_first / (jnp.sqrt(new_second) + 1e-08)
    shift_by = jnp.left_shift(jnp.int32(1), exponent[0].astype(jnp.int32))
    source = (jnp.arange(REPLICAS, dtype=jnp.int32) - shift_by) % REPLICAS
    mixed_param = 0.5 * stepped + 0.5 * stepped[source]
    mixed_weight = 0.5 * push_weight + 0.5 * push_weight[source]
    return (mixed_param, new_first, new_second, mixed_weight)
```

```python
from functools import partial

import jax
import jax.numpy as jnp
from jax import lax
from jax.experimental import pallas as pl
from jax.experimental.pallas import tpu as pltpu
from jax.sharding import PartitionSpec as P

X_WIDTH = 4096
Y_WIDTH = 4096
PIECE = 2048
LIMIT = 32 * 1024 * 1024
ANY = pl.BlockSpec(memory_space=pl.ANY)


def call(kernel, width, tile, ins, outs, after=(), aliases=None, cost=1, limit=LIMIT):
    specs, operands = [], []
    for array, start in ins:
        rows, columns = array.shape
        operands.append(array)
        if start is None:
            specs.append(pl.BlockSpec((rows, columns), lambda j: (0, 0)))
        else:
            specs.append(pl.BlockSpec((rows, tile), lambda j, s=start // tile: (0, j + s)))
    out_specs, shapes = [], []
    for rows, columns, start in outs:
        out_specs.append(pl.BlockSpec((rows, tile), lambda j, s=start // tile: (0, j + s)))
        shapes.append(jax.ShapeDtypeStruct((rows, columns), jnp.float32))
    count, skipped = len(ins), len(after)
    pairs = {}
    for out, array in (aliases or {}).items():
        pairs[count + skipped + len(pairs)] = out
    extra = list(after) + list((aliases or {}).values())

    def wrapped(*refs):
        kernel(*refs[:count], *refs[count + len(extra) :])

    return pl.pallas_call(
        wrapped,
        grid=(width // tile,),
        in_specs=specs + [ANY] * len(extra),
        out_specs=out_specs,
        out_shape=shapes,
        input_output_aliases=pairs,
        compiler_params=pltpu.CompilerParams(vmem_limit_bytes=limit),
        cost_estimate=pl.CostEstimate(flops=0, bytes_accessed=cost * 3_000_000, transcendentals=0),
    )(*operands, *extra)


def strips(rows, step, work):
    def one(i, carry):
        work(pl.ds(pl.multiple_of(i * step, step), step))
        return carry

    lax.fori_loop(0, rows // step, one, 0)


def product(cot, acts, start, width, after=(), limit=LIMIT):
    rows, tokens = cot.shape

    def kernel(c_ref, a_ref, o_ref):
        o_ref[...] = jnp.dot(c_ref[...], a_ref[...], preferred_element_type=jnp.float32)

    return call(
        kernel, width, 1024, [(cot, None), (acts, start)], [(rows, width, 0)], after, limit=limit
    )[0]


def product_add(
    cot, acts, peer, start, kind, after, whole, out_start, held=None
):
    rows, tokens = cot.shape

    def kernel(c_ref, a_ref, p_ref, *o_refs):
        total = jnp.dot(c_ref[...], a_ref[...], preferred_element_type=jnp.float32) + p_ref[...]
        if kind == "y":
            o_refs[0][...] = total[:128]
            o_refs[1][...] = total[128:]
        else:
            for d in range(4):
                o_refs[d][:32] = total[32 * d : 32 * d + 32]
                o_refs[d][32:] = total[128 + 32 * d : 160 + 32 * d]

    outs = [(128, whole, out_start)] * 2 if kind == "y" else [(64, whole, out_start)] * 4
    return call(
        kernel, peer.shape[1], 1024, [(cot, None), (acts, start), (peer, 0)], outs, after,
        dict(enumerate(held)) if held else None,
    )


def add_split(own, peer, after, whole, out_start, held=None):
    width = own.shape[1]

    def kernel(a_ref, b_ref, *o_refs):
        for d in range(4):
            def work(at, d=d):
                from_at = pl.ds(at.start + 32 * d, at.size)
                o_refs[d][at] = a_ref[from_at] + b_ref[from_at]

            strips(32, 8, work)

    return call(
        kernel, width, 2048, [(own, 0), (peer, 0)], [(32, whole, out_start)] * 4, after,
        dict(enumerate(held)) if held else None,
    )


def sum_split(terms, after=()):
    width = terms[0].shape[1]

    def kernel(a_ref, b_ref, c_ref, d_ref, *o_refs):
        for i in range(2):
            def work(at, i=i):
                from_at = pl.ds(at.start + 32 * i, at.size)
                o_refs[i][at] = (a_ref[from_at] + b_ref[from_at]) + (c_ref[from_at] + d_ref[from_at])

            strips(32, 8, work)

    return call(kernel, width, 2048, [(t, 0) for t in terms], [(32, width, 0)] * 2, after, None, 30)


def adam(terms, param, first, second, held, start, width, whole, step_start, after=()):
    count, columns = len(terms), param.shape[1]

    def kernel(*refs):
        param_ref, first_ref, second_ref = refs[count : count + 3]
        step_ref, new_first_ref, new_second_ref = refs[-3:]

        def work(at):
            grad = refs[0][at]
            for ref in refs[1:count]:
                grad = grad + ref[at]
            new_first = 0.9 * first_ref[at] + 0.1 * grad
            new_second = 0.999 * second_ref[at] + 0.001 * grad * grad
            new_first_ref[at] = new_first
            new_second_ref[at] = new_second
            step_ref[at] = param_ref[at] - 0.1 * (new_first / (jnp.sqrt(new_second) + 1e-08))

        strips(32, 8, work)

    ins = [(t, 0) for t in terms] + [(a, start) for a in (param, first, second)]
    outs = [(32, whole, step_start), (32, columns, start), (32, columns, start)]
    return call(kernel, width, 2048, ins, outs, after, held)


def to_core(value):
    return lax.ppermute(value, "fsdp", [(i, i ^ 1) for i in range(16)])


def to_y(value):
    return lax.ppermute(value, "fsdp", [(i, i ^ 8) for i in range(16)])


def to_x(value, by):
    return lax.ppermute(
        value, "fsdp", [(i, (i & 9) | ((((i >> 1) + by) & 3) << 1)) for i in range(16)]
    )


def to_rep(value, by):
    return lax.ppermute(value, "rep", [(i, (i + by) % 16) for i in range(16)])


def dealt(cot):
    me = lax.axis_index("fsdp")
    at = lax.broadcasted_iota(jnp.int32, (512, 512), 0)
    rel = lax.broadcasted_iota(jnp.int32, (512, 512), 1)
    to = rel >> 5
    core = (me ^ 1 ^ (to >> 3)) & 1
    y = ((me >> 3) ^ (to >> 2)) & 1
    x = ((me >> 1) + to) & 3
    source = (y * 8 + x * 2 + core) * 32 + (rel & 31)
    pick = (at == source).astype(cot.dtype)
    return lax.dot_general(
        pick, cot, (((0,), (1,)), ((), ())), preferred_element_type=jnp.float32
    ).astype(cot.dtype)


def pushed(operands, power):
    return [to_rep(value, 2**power) for value in operands]


def push(exponent, operands):
    return lax.switch(exponent, [partial(pushed, power=p) for p in range(4)], operands)


def body(param, first, second, push_weight, acts, cotangent, exponent):
    cot = dealt(cotangent[0])
    theirs, mine = cot[:256], cot[256:]
    param, first, second, acts = param[0], first[0], second[0], acts[0]
    columns = param.shape[1]
    order = (1, 3, 2)

    cuts = range(0, columns, PIECE)
    outs, ins = [], []
    for start in cuts:
        outs.append(product(theirs, acts, start, PIECE, outs[-1:]))
        ins.append(to_core(outs[-1]))
    parts_x, after = None, outs[-1:]
    for start in cuts[: X_WIDTH // PIECE]:
        parts_x = product_add(
            mine, acts, ins[start // PIECE], start, "x", after, X_WIDTH, start, parts_x
        )
        after = []
    sum_x = [to_x(parts_x[d], d) for d in order]
    after, parts_y, peer_y = parts_x[:1], [], []
    for start in cuts[X_WIDTH // PIECE :]:
        parts_y.append(
            product_add(mine, acts, ins[start // PIECE], start, "y", after, PIECE, 0)
        )
        after = parts_y[-1][:1]
        peer_y.append(to_y(parts_y[-1][1]))

    halves_x = sum_split([parts_x[0]] + sum_x, after)
    last_x = to_y(halves_x[1])
    blocks_y, after = None, halves_x[:1]
    for i, (parts, peer) in enumerate(zip(parts_y, peer_y)):
        blocks_y = add_split(parts[0], peer, after, Y_WIDTH, i * PIECE, blocks_y)
        after = []
    last_y = [to_x(blocks_y[d], d) for d in order]
    step_x, new_first, new_second = adam(
        [halves_x[0], last_x], param, first, second, None, 0, X_WIDTH, X_WIDTH, 0, [blocks_y[0]]
    )
    peer_x, weight_peer = push(exponent[0], (step_x, push_weight))
    step_y, new_first, new_second = adam(
        [blocks_y[0]] + last_y, param, first, second, {1: new_first, 2: new_second},
        X_WIDTH, Y_WIDTH, Y_WIDTH, 0, [peer_x],
    )
    (peer_y,) = push(exponent[0], (step_y,))
    mixed = jnp.concatenate(
        [0.5 * step_x + 0.5 * peer_x, 0.5 * step_y + 0.5 * peer_y], axis=1
    )
    weight = 0.5 * push_weight + 0.5 * weight_peer
    return mixed[None], new_first[None], new_second[None], weight


def solution(mesh):
    return jax.shard_map(
        body,
        mesh=mesh,
        in_specs=(
            P("rep", "fsdp", None),
            P("rep", "fsdp", None),
            P("rep", "fsdp", None),
            P("rep"),
            P("rep", "fsdp", None),
            P("rep", "fsdp", None),
            P(),
        ),
        out_specs=(
            P("rep", "fsdp", None),
            P("rep", "fsdp", None),
            P("rep", "fsdp", None),
            P("rep"),
        ),
        check_vma=False,
    )
```

```python
from functools import partial

import jax
import jax.numpy as jnp
from jax import lax
from jax.experimental import pallas as pl
from jax.experimental.pallas import tpu as pltpu
from jax.sharding import PartitionSpec as P

X_WIDTH = 2560
Y_WIDTH = 3072
HALF = X_WIDTH // 2
TILE = 1024
COST = (0.1, 2, 0.1, 0.1, 0.1, 0.8, 0.01)
LIMIT = 16 * 1024 * 1024
ANY = pl.BlockSpec(memory_space=pl.ANY)
HELD = pl.BlockSpec(memory_space=pltpu.HBM)


def call(kernel, width, tile, ins, outs, after=(), aliases=None, cost=0.1, limit=LIMIT):
    specs, operands = [], []
    for array, start in ins:
        rows, columns = array.shape
        operands.append(array)
        if start is None:
            specs.append(pl.BlockSpec((rows, columns), lambda j: (0, 0)))
        else:
            specs.append(pl.BlockSpec((rows, tile), lambda j, s=start // tile: (0, j + s)))
    out_specs, shapes = [], []
    for rows, columns, start in outs:
        if start is None:
            out_specs.append(pl.BlockSpec((rows, columns), lambda j: (0, 0)))
        else:
            out_specs.append(pl.BlockSpec((rows, tile), lambda j, s=start // tile: (0, j + s)))
        shapes.append(jax.ShapeDtypeStruct((rows, columns), jnp.float32))
    count, skipped = len(ins), len(after)
    pairs = {}
    for out, array in (aliases or {}).items():
        pairs[count + skipped + len(pairs)] = out
    extra = list(after) + list((aliases or {}).values())

    def wrapped(*refs):
        kernel(*refs[:count], *refs[count + len(extra) :])

    return pl.pallas_call(
        wrapped,
        grid=(width // tile,),
        in_specs=specs + [ANY] * skipped + [HELD] * len(pairs),
        out_specs=out_specs,
        out_shape=shapes,
        input_output_aliases=pairs,
        compiler_params=pltpu.CompilerParams(vmem_limit_bytes=limit),
        cost_estimate=pl.CostEstimate(flops=int(cost * 1.15e9), bytes_accessed=int(cost * 3e6), transcendentals=0),
    )(*operands, *extra)


def strips(rows, step, work):
    def one(i, carry):
        work(pl.ds(pl.multiple_of(i * step, step), step))
        return carry

    lax.fori_loop(0, rows // step, one, 0)


def product(cot, acts, start, width, tile, after=()):
    def kernel(c_ref, a_ref, o_ref):
        o_ref[...] = jnp.dot(c_ref[...], a_ref[...], preferred_element_type=jnp.float32)

    return call(kernel, width, tile, [(cot, None), (acts, start)], [(256, width, 0)], after)[0]


def product_add_y(cot, acts, peer, start, after):
    def kernel(c_ref, a_ref, p_ref, stay_ref, go_ref):
        total = jnp.dot(c_ref[...], a_ref[...], preferred_element_type=jnp.float32) + p_ref[...]
        stay_ref[...] = total[:128]
        go_ref[...] = total[128:]

    return call(
        kernel, Y_WIDTH, TILE, [(cot, None), (acts, start), (peer, 0)], [(128, Y_WIDTH, 0)] * 2, after
    )


def product_add_x(cot, acts, peer, start, after):
    def kernel(c_ref, a_ref, p_ref, *o_refs):
        total = jnp.dot(c_ref[...], a_ref[...], preferred_element_type=jnp.float32) + p_ref[...]

        def put(ref, d):
            ref[:32] = total[32 * d : 32 * d + 32]
            ref[32:] = total[128 + 32 * d : 160 + 32 * d]

        put(o_refs[0], 0)
        put(o_refs[1], 1)
        put(o_refs[2], 3)
        for side in range(2):
            pl.when(pl.program_id(0) == side)(partial(put, o_refs[3 + side], 2))

    outs = [(64, X_WIDTH, 0)] * 3 + [(64, HALF, None)] * 2
    return call(kernel, X_WIDTH, HALF, [(cot, None), (acts, start), (peer, 0)], outs, after)


def relay_add(parts, from_left, from_right, after, cost):
    def kernel(a_ref, b_ref, c_ref, d_ref, right_ref, left_ref):
        def work(at):
            right_ref[at] = a_ref[at] + b_ref[at]
            left_ref[at] = c_ref[at] + d_ref[at]

        strips(64, 8, work)

    half = pl.BlockSpec((64, HALF), lambda j: (0, 0))
    other = pl.BlockSpec((64, HALF), lambda j: (0, 1))
    extra = list(after)
    return pl.pallas_call(
        lambda *refs: kernel(*refs[:4], *refs[-2:]),
        grid=(1,),
        in_specs=[half, half, other, half] + [ANY] * len(extra),
        out_specs=[half, other],
        out_shape=[jax.ShapeDtypeStruct((64, X_WIDTH), jnp.float32)] * 2,
        input_output_aliases={0: 0, 2: 1},
        compiler_params=pltpu.CompilerParams(vmem_limit_bytes=LIMIT),
        cost_estimate=pl.CostEstimate(flops=int(cost * 1.15e9), bytes_accessed=int(cost * 3e6), transcendentals=0),
    )(parts[1], from_left, parts[2], from_right, *extra)


def add_split(own, peer, after, cost):
    def kernel(a_ref, b_ref, *o_refs):
        for d in range(4):
            def work(at, d=d):
                from_at = pl.ds(at.start + 32 * d, at.size)
                o_refs[d][at] = a_ref[from_at] + b_ref[from_at]

            strips(32, 8, work)

    return call(
        kernel, Y_WIDTH, TILE, [(own, 0), (peer, 0)], [(32, Y_WIDTH, 0)] * 4, after, cost=cost
    )


def sum_split(terms, after, cost):
    def kernel(a_ref, b_ref, c_ref, *o_refs):
        for i in range(2):
            def work(at, i=i):
                from_at = pl.ds(at.start + 32 * i, at.size)
                o_refs[i][at] = a_ref[from_at] + (b_ref[from_at] + c_ref[from_at])

            strips(32, 8, work)

    return call(kernel, X_WIDTH, HALF, [(t, 0) for t in terms], [(32, X_WIDTH, 0)] * 2, after, cost=cost)


def adam(terms, param, first, second, held, start, tile, whole, after, cost):
    count, columns, width = len(terms), param.shape[1], terms[0].shape[1]

    def kernel(*refs):
        param_ref, first_ref, second_ref = refs[count : count + 3]
        step_ref, new_first_ref, new_second_ref = refs[-3:]

        def work(at):
            grad = refs[0][at]
            for ref in refs[1:count]:
                grad = grad + ref[at]
            new_first = 0.9 * first_ref[at] + 0.1 * grad
            new_second = 0.999 * second_ref[at] + 0.001 * grad * grad
            new_first_ref[at] = new_first
            new_second_ref[at] = new_second
            step_ref[at] = param_ref[at] - 0.1 * (new_first / (jnp.sqrt(new_second) + 1e-08))

        strips(32, 8, work)

    ins = [(t, 0) for t in terms] + [(a, start) for a in (param, first, second)]
    outs = [(32, whole, start if start < whole else 0), (32, columns, start), (32, columns, start)]
    return call(kernel, width, tile, ins, outs, after, held, cost=cost)


def mix(step, peer, held, start, tile, columns):
    def kernel(a_ref, b_ref, o_ref):
        def work(at):
            o_ref[at] = 0.5 * a_ref[at] + 0.5 * b_ref[at]

        strips(32, 8, work)

    return call(
        kernel, step.shape[1], tile, [(step, 0), (peer, 0)], [(32, columns, start)], (),
        None if held is None else {0: held},
    )[0]


def to_core(value):
    return lax.ppermute(value, "fsdp", [(i, i ^ 1) for i in range(16)])


def to_y(value):
    return lax.ppermute(value, "fsdp", [(i, i ^ 8) for i in range(16)])


def to_x(value, by):
    return lax.ppermute(
        value, "fsdp", [(i, (i & 9) | ((((i >> 1) + by) & 3) << 1)) for i in range(16)]
    )


def to_rep(value, by):
    return lax.ppermute(value, "rep", [(i, (i + by) % 16) for i in range(16)])


def dealt(cot):
    me = lax.axis_index("fsdp")
    at = lax.broadcasted_iota(jnp.int32, (512, 512), 0)
    rel = lax.broadcasted_iota(jnp.int32, (512, 512), 1)
    to = rel >> 5
    core = (me ^ 1 ^ (to >> 3)) & 1
    y = ((me >> 3) ^ (to >> 2)) & 1
    x = ((me >> 1) + to) & 3
    source = (y * 8 + x * 2 + core) * 32 + (rel & 31)
    pick = (at == source).astype(cot.dtype)
    return lax.dot_general(
        pick, cot, (((0,), (1,)), ((), ())), preferred_element_type=jnp.float32
    ).astype(cot.dtype)


def push(exponent, values, work, *rest):
    def branch(power, operands):
        got = [to_rep(value, 2**power) for value in operands[0]]
        return got, work(*operands[1])

    return lax.switch(exponent, [partial(branch, p) for p in range(4)], (values, rest))


def body(param, first, second, push_weight, acts, cotangent, exponent):
    cot = dealt(cotangent[0])
    theirs, mine = cot[:256], cot[256:]
    param, first, second, acts = param[0], first[0], second[0], acts[0]
    columns = param.shape[1]
    order = (1, 3, 2)

    b, y = X_WIDTH, 2 * X_WIDTH
    out_y = product(theirs, acts, y, Y_WIDTH, TILE)
    in_y = to_core(out_y)
    out_0 = product(theirs, acts, 0, X_WIDTH, HALF, [out_y])
    in_0 = to_core(out_0)
    out_1 = product(theirs, acts, b, X_WIDTH, HALF, [out_0])
    in_1 = to_core(out_1)
    y_2 = product_add_y(mine, acts, in_y, y, [out_1])
    peer_2 = to_y(y_2[1])
    x_0 = product_add_x(mine, acts, in_0, 0, y_2[:1])
    left_0, right_0 = to_x(x_0[3], 1), to_x(x_0[4], 3)
    x_1 = product_add_x(mine, acts, in_1, b, x_0[:1])
    left_1, right_1 = to_x(x_1[3], 1), to_x(x_1[4], 3)
    both_0 = relay_add(x_0, left_0, right_0, x_1[:1], COST[0])
    from_0 = [to_x(both_0[0], 1), to_x(both_0[1], 3)]
    both_1 = relay_add(x_1, left_1, right_1, both_0[:1], COST[1])
    from_1 = [to_x(both_1[0], 1), to_x(both_1[1], 3)]
    halves_0 = sum_split([x_0[0]] + from_0, both_1[:1], COST[2])
    last_0 = to_y(halves_0[1])
    blocks = add_split(y_2[0], peer_2, halves_0[:1], COST[3])
    last = [to_x(blocks[d], d) for d in order]
    halves_1 = sum_split([x_1[0]] + from_1, blocks[:1], COST[4])
    last_1 = to_y(halves_1[1])
    moments = (param, first, second)
    step, *held = adam(
        [halves_0[0], last_0], *moments, None, 0, X_WIDTH, y, halves_1[:1], COST[5]
    )
    held = {0: step, 1: held[0], 2: held[1]}
    step, *held = adam([halves_1[0], last_1], *moments, held, b, X_WIDTH, y, [], COST[6])
    (got, weight_peer), _ = push(exponent[0], [step, push_weight], lambda: ())
    held = {1: held[0], 2: held[1]}
    step_2, *held = adam([blocks[0]] + last, *moments, held, y, TILE, Y_WIDTH, [got], 1)
    (got_2,), mixed = push(
        exponent[0], [step_2], lambda *v: mix(*v, None, 0, X_WIDTH, columns), step, got
    )
    mixed = mix(step_2, got_2, mixed, y, TILE, columns)
    new_first, new_second = held
    weight = 0.5 * push_weight + 0.5 * weight_peer
    return mixed[None], new_first[None], new_second[None], weight


def solution(mesh):
    return jax.shard_map(
        body,
        mesh=mesh,
        in_specs=(
            P("rep", "fsdp", None),
            P("rep", "fsdp", None),
            P("rep", "fsdp", None),
            P("rep"),
            P("rep", "fsdp", None),
            P("rep", "fsdp", None),
            P(),
        ),
        out_specs=(
            P("rep", "fsdp", None),
            P("rep", "fsdp", None),
            P("rep", "fsdp", None),
            P("rep"),
        ),
        check_vma=False,
    )
```

```python
from functools import partial

import jax
import jax.numpy as jnp
from jax import lax
from jax.experimental import pallas as pl
from jax.experimental.pallas import tpu as pltpu
from jax.sharding import PartitionSpec as P

PIECE = 2048
HALF = PIECE // 2
COST = (0.5, 0.1, 6, 1, 0.1, 0.1, 20, 10, 1, 1)
LIMIT = 16 * 1024 * 1024
ANY = pl.BlockSpec(memory_space=pl.ANY)
HELD = pl.BlockSpec(memory_space=pltpu.HBM)


def call(kernel, width, tile, ins, outs, after=(), aliases=None, cost=0.1, limit=LIMIT):
    specs, operands = [], []
    for array, start in ins:
        rows, columns = array.shape
        operands.append(array)
        if start is None:
            specs.append(pl.BlockSpec((rows, columns), lambda j: (0, 0)))
        else:
            specs.append(pl.BlockSpec((rows, tile), lambda j, s=start // tile: (0, j + s)))
    out_specs, shapes = [], []
    for rows, columns, start in outs:
        if start is None:
            out_specs.append(pl.BlockSpec((rows, columns), lambda j: (0, 0)))
        else:
            out_specs.append(pl.BlockSpec((rows, tile), lambda j, s=start // tile: (0, j + s)))
        shapes.append(jax.ShapeDtypeStruct((rows, columns), jnp.float32))
    count, skipped = len(ins), len(after)
    pairs = {}
    for out, array in (aliases or {}).items():
        pairs[count + skipped + len(pairs)] = out
    extra = list(after) + list((aliases or {}).values())

    def wrapped(*refs):
        kernel(*refs[:count], *refs[count + len(extra) :])

    return pl.pallas_call(
        wrapped,
        grid=(width // tile,),
        in_specs=specs + [ANY] * skipped + [HELD] * len(pairs),
        out_specs=out_specs,
        out_shape=shapes,
        input_output_aliases=pairs,
        compiler_params=pltpu.CompilerParams(vmem_limit_bytes=limit),
        cost_estimate=pl.CostEstimate(flops=int(cost * 1.15e9), bytes_accessed=int(cost * 3e6), transcendentals=0),
    )(*operands, *extra)


def strips(rows, step, work):
    def one(i, carry):
        work(pl.ds(pl.multiple_of(i * step, step), step))
        return carry

    lax.fori_loop(0, rows // step, one, 0)


def product(cot, acts, start, width, after=(), limit=LIMIT):
    rows, tokens = cot.shape

    def kernel(c_ref, a_ref, o_ref):
        o_ref[...] = jnp.dot(c_ref[...], a_ref[...], preferred_element_type=jnp.float32)

    return call(
        kernel, width, 1024, [(cot, None), (acts, start)], [(rows, width, 0)], after, limit=limit
    )[0]


def product_add_y(cot, acts, peer, start, after):
    def kernel(c_ref, a_ref, p_ref, stay_ref, go_ref):
        total = jnp.dot(c_ref[...], a_ref[...], preferred_element_type=jnp.float32) + p_ref[...]
        stay_ref[...] = total[:128]
        go_ref[...] = total[128:]

    return call(
        kernel, PIECE, HALF, [(cot, None), (acts, start), (peer, 0)], [(128, PIECE, 0)] * 2, after
    )


def product_add_x(cot, acts, peer, start, after):
    def kernel(c_ref, a_ref, p_ref, *o_refs):
        total = jnp.dot(c_ref[...], a_ref[...], preferred_element_type=jnp.float32) + p_ref[...]

        def put(ref, d):
            ref[:32] = total[32 * d : 32 * d + 32]
            ref[32:] = total[128 + 32 * d : 160 + 32 * d]

        put(o_refs[0], 0)
        put(o_refs[1], 1)
        put(o_refs[2], 3)
        for side in range(2):
            pl.when(pl.program_id(0) == side)(partial(put, o_refs[3 + side], 2))

    outs = [(64, PIECE, 0)] * 3 + [(64, HALF, None)] * 2
    return call(kernel, PIECE, HALF, [(cot, None), (acts, start), (peer, 0)], outs, after)


def relay_add(parts, from_left, from_right, after, cost):
    def kernel(a_ref, b_ref, c_ref, d_ref, right_ref, left_ref):
        def work(at):
            right_ref[at] = a_ref[at] + b_ref[at]
            left_ref[at] = c_ref[at] + d_ref[at]

        strips(64, 8, work)

    half = pl.BlockSpec((64, HALF), lambda j: (0, 0))
    other = pl.BlockSpec((64, HALF), lambda j: (0, 1))
    extra = list(after)
    return pl.pallas_call(
        lambda *refs: kernel(*refs[:4], *refs[-2:]),
        grid=(1,),
        in_specs=[half, half, other, half] + [ANY] * len(extra),
        out_specs=[half, other],
        out_shape=[jax.ShapeDtypeStruct((64, PIECE), jnp.float32)] * 2,
        input_output_aliases={0: 0, 2: 1},
        compiler_params=pltpu.CompilerParams(vmem_limit_bytes=LIMIT),
        cost_estimate=pl.CostEstimate(flops=int(cost * 1.15e9), bytes_accessed=int(cost * 3e6), transcendentals=0),
    )(parts[1], from_left, parts[2], from_right, *extra)


def add_split(own, peer, after, cost):
    def kernel(a_ref, b_ref, *o_refs):
        for d in range(4):
            def work(at, d=d):
                from_at = pl.ds(at.start + 32 * d, at.size)
                o_refs[d][at] = a_ref[from_at] + b_ref[from_at]

            strips(32, 8, work)

    return call(
        kernel, PIECE, HALF, [(own, 0), (peer, 0)], [(32, PIECE, 0)] * 4, after, cost=cost
    )


def sum_split(terms, after, out_start, held, cost):
    def kernel(a_ref, b_ref, c_ref, *o_refs):
        for i in range(2):
            def work(at, i=i):
                from_at = pl.ds(at.start + 32 * i, at.size)
                o_refs[i][at] = a_ref[from_at] + (b_ref[from_at] + c_ref[from_at])

            strips(32, 8, work)

    return call(
        kernel, PIECE, HALF, [(t, 0) for t in terms], [(32, 2 * PIECE, out_start)] * 2, after,
        None if held is None else dict(enumerate(held)), cost=cost,
    )


def adam(terms, param, first, second, held, start, width, whole, step_start, after, cost):
    count, columns = len(terms), param.shape[1]

    def kernel(*refs):
        param_ref, first_ref, second_ref = refs[count : count + 3]
        step_ref, new_first_ref, new_second_ref = refs[-3:]

        def work(at):
            grad = refs[0][at]
            for ref in refs[1:count]:
                grad = grad + ref[at]
            new_first = 0.9 * first_ref[at] + 0.1 * grad
            new_second = 0.999 * second_ref[at] + 0.001 * grad * grad
            new_first_ref[at] = new_first
            new_second_ref[at] = new_second
            step_ref[at] = param_ref[at] - 0.1 * (new_first / (jnp.sqrt(new_second) + 1e-08))

        strips(32, 8, work)

    ins = [(t, 0) for t in terms] + [(a, start) for a in (param, first, second)]
    outs = [(32, whole, step_start), (32, columns, start), (32, columns, start)]
    return call(kernel, width, PIECE, ins, outs, after, held, cost=cost)


def mix(step, peer, held, start, columns):
    def kernel(a_ref, b_ref, o_ref):
        def work(at):
            o_ref[at] = 0.5 * a_ref[at] + 0.5 * b_ref[at]

        strips(32, 8, work)

    return call(
        kernel, step.shape[1], PIECE, [(step, 0), (peer, 0)], [(32, columns, start)], (),
        None if held is None else {0: held},
    )[0]


def to_core(value):
    return lax.ppermute(value, "fsdp", [(i, i ^ 1) for i in range(16)])


def to_y(value):
    return lax.ppermute(value, "fsdp", [(i, i ^ 8) for i in range(16)])


def to_x(value, by):
    return lax.ppermute(
        value, "fsdp", [(i, (i & 9) | ((((i >> 1) + by) & 3) << 1)) for i in range(16)]
    )


def to_rep(value, by):
    return lax.ppermute(value, "rep", [(i, (i + by) % 16) for i in range(16)])


def dealt(cot):
    me = lax.axis_index("fsdp")
    at = lax.broadcasted_iota(jnp.int32, (512, 512), 0)
    rel = lax.broadcasted_iota(jnp.int32, (512, 512), 1)
    to = rel >> 5
    core = (me ^ 1 ^ (to >> 3)) & 1
    y = ((me >> 3) ^ (to >> 2)) & 1
    x = ((me >> 1) + to) & 3
    source = (y * 8 + x * 2 + core) * 32 + (rel & 31)
    pick = (at == source).astype(cot.dtype)
    return lax.dot_general(
        pick, cot, (((0,), (1,)), ((), ())), preferred_element_type=jnp.float32
    ).astype(cot.dtype)


def push(exponent, values, work, *rest):
    def branch(power, operands):
        got = [to_rep(value, 2**power) for value in operands[0]]
        return got, work(*operands[1])

    return lax.switch(exponent, [partial(branch, p) for p in range(4)], (values, rest))


def body(param, first, second, push_weight, acts, cotangent, exponent):
    cot = dealt(cotangent[0])
    theirs, mine = cot[:256], cot[256:]
    param, first, second, acts = param[0], first[0], second[0], acts[0]
    columns = param.shape[1]
    order = (1, 3, 2)

    outs, peers, pieces = {}, {}, {}
    for i in (2, 0, 1, 3):
        before = list(outs.values())[-1:]
        acts, *before = lax.optimization_barrier((acts, *before))
        pieces[i] = acts[:, i * PIECE : (i + 1) * PIECE]
        outs[i] = product(theirs, pieces[i], 0, PIECE, before)
        peers[i] = to_core(outs[i])
    y_2 = product_add_y(mine, pieces[2], peers[2], 0, [outs[3]])
    peer_2 = to_y(y_2[1])
    x_0 = product_add_x(mine, pieces[0], peers[0], 0, y_2[:1])
    left_0, right_0 = to_x(x_0[3], 1), to_x(x_0[4], 3)
    x_1 = product_add_x(mine, pieces[1], peers[1], 0, x_0[:1])
    left_1, right_1 = to_x(x_1[3], 1), to_x(x_1[4], 3)
    both_0 = relay_add(x_0, left_0, right_0, x_1[:1], COST[0])
    in_0 = [to_x(both_0[0], 1), to_x(both_0[1], 3)]
    y_3 = product_add_y(mine, pieces[3], peers[3], 0, both_0[:1])
    peer_3 = to_y(y_3[1])
    both_1 = relay_add(x_1, left_1, right_1, y_3[:1], COST[1])
    in_1 = [to_x(both_1[0], 1), to_x(both_1[1], 3)]
    blocks_2 = add_split(y_2[0], peer_2, both_1[:1], COST[2])
    last_2 = [to_x(blocks_2[d], d) for d in order]
    halves = sum_split([x_0[0]] + in_0, blocks_2[:1], 0, None, COST[3])
    halves = sum_split([x_1[0]] + in_1, [], PIECE, halves, COST[4])
    last_0 = to_y(halves[1])
    blocks_3 = add_split(y_3[0], peer_3, halves[:1], COST[5])
    last_3 = [to_x(blocks_3[d], d) for d in order]
    moments = (param, first, second)
    step_2, *held = adam(
        [blocks_2[0]] + last_2, *moments, None, 2 * PIECE, PIECE, PIECE, 0, blocks_3[:1], COST[6]
    )
    (got_2,), _ = push(exponent[0], [step_2], lambda: ())
    step_0, *held = adam(
        [halves[0], last_0], *moments, {1: held[0], 2: held[1]}, 0, 2 * PIECE, 2 * PIECE, 0, [got_2],
        COST[7],
    )
    def finish(own, others, held, before, got):
        later = adam(
            [own] + others, *moments, {1: held[0], 2: held[1]}, 3 * PIECE, PIECE, PIECE, 0, [], COST[8]
        )
        return later, mix(before, got, None, 2 * PIECE, columns)

    (got_0, weight_peer), ((step_3, *held), mixed) = push(
        exponent[0], [step_0, push_weight], finish, blocks_3[0], last_3, held, step_2, got_2
    )
    (got_3,), mixed = push(
        exponent[0], [step_3], lambda *v: mix(*v, 0, columns), step_0, got_0, mixed
    )
    mixed = mix(step_3, got_3, mixed, 3 * PIECE, columns)
    new_first, new_second = held
    weight = 0.5 * push_weight + 0.5 * weight_peer
    return mixed[None], new_first[None], new_second[None], weight


def solution(mesh):
    return jax.shard_map(
        body,
        mesh=mesh,
        in_specs=(
            P("rep", "fsdp", None),
            P("rep", "fsdp", None),
            P("rep", "fsdp", None),
            P("rep"),
            P("rep", "fsdp", None),
            P("rep", "fsdp", None),
            P(),
        ),
        out_specs=(
            P("rep", "fsdp", None),
            P("rep", "fsdp", None),
            P("rep", "fsdp", None),
            P("rep"),
        ),
        check_vma=False,
    )
```

```python
from functools import partial

import jax
import jax.numpy as jnp
from jax import lax
from jax.experimental import pallas as pl
from jax.experimental.pallas import tpu as pltpu
from jax.sharding import PartitionSpec as P

PIECE = 2048
HALF = PIECE // 2
COST = (0.5, 0.1, 6, 1, 0.1, 0.1, 20, 10, 1, 1)
LIMIT = 16 * 1024 * 1024
ANY = pl.BlockSpec(memory_space=pl.ANY)
HELD = pl.BlockSpec(memory_space=pltpu.HBM)


def call(kernel, width, tile, ins, outs, after=(), aliases=None, cost=0.1, limit=LIMIT):
    specs, operands = [], []
    for array, start in ins:
        rows, columns = array.shape
        operands.append(array)
        if start is None:
            specs.append(pl.BlockSpec((rows, columns), lambda j: (0, 0)))
        else:
            specs.append(pl.BlockSpec((rows, tile), lambda j, s=start // tile: (0, j + s)))
    out_specs, shapes = [], []
    for rows, columns, start in outs:
        if start is None:
            out_specs.append(pl.BlockSpec((rows, columns), lambda j: (0, 0)))
        else:
            out_specs.append(pl.BlockSpec((rows, tile), lambda j, s=start // tile: (0, j + s)))
        shapes.append(jax.ShapeDtypeStruct((rows, columns), jnp.float32))
    count, skipped = len(ins), len(after)
    pairs = {}
    for out, array in (aliases or {}).items():
        pairs[count + skipped + len(pairs)] = out
    extra = list(after) + list((aliases or {}).values())

    def wrapped(*refs):
        kernel(*refs[:count], *refs[count + len(extra) :])

    return pl.pallas_call(
        wrapped,
        grid=(width // tile,),
        in_specs=specs + [ANY] * skipped + [HELD] * len(pairs),
        out_specs=out_specs,
        out_shape=shapes,
        input_output_aliases=pairs,
        compiler_params=pltpu.CompilerParams(vmem_limit_bytes=limit),
        cost_estimate=pl.CostEstimate(flops=int(cost * 1.15e9), bytes_accessed=int(cost * 3e6), transcendentals=0),
    )(*operands, *extra)


def strips(rows, step, work):
    def one(i, carry):
        work(pl.ds(pl.multiple_of(i * step, step), step))
        return carry

    lax.fori_loop(0, rows // step, one, 0)


def product(cot, acts, start, width, after=(), limit=LIMIT):
    rows, tokens = cot.shape

    def kernel(c_ref, a_ref, o_ref):
        o_ref[...] = jnp.dot(c_ref[...], a_ref[...], preferred_element_type=jnp.float32)

    return call(
        kernel, width, 1024, [(cot, None), (acts, start)], [(rows, width, 0)], after, limit=limit
    )[0]


def product_add_y(cot, acts, peer, start, after):
    def kernel(c_ref, a_ref, p_ref, stay_ref, go_ref):
        total = jnp.dot(c_ref[...], a_ref[...], preferred_element_type=jnp.float32) + p_ref[...]
        stay_ref[...] = total[:128]
        go_ref[...] = total[128:]

    return call(
        kernel, PIECE, HALF, [(cot, None), (acts, start), (peer, 0)], [(128, PIECE, 0)] * 2, after
    )


def product_add_x(cot, acts, peer, start, after):
    def kernel(c_ref, a_ref, p_ref, *o_refs):
        total = jnp.dot(c_ref[...], a_ref[...], preferred_element_type=jnp.float32) + p_ref[...]

        def put(ref, d):
            ref[:32] = total[32 * d : 32 * d + 32]
            ref[32:] = total[128 + 32 * d : 160 + 32 * d]

        put(o_refs[0], 0)
        put(o_refs[1], 1)
        put(o_refs[2], 3)
        for side in range(2):
            pl.when(pl.program_id(0) == side)(partial(put, o_refs[3 + side], 2))

    outs = [(64, PIECE, 0)] * 3 + [(64, HALF, None)] * 2
    return call(kernel, PIECE, HALF, [(cot, None), (acts, start), (peer, 0)], outs, after)


def relay_add(parts, from_left, from_right, after, cost):
    def kernel(a_ref, b_ref, c_ref, d_ref, right_ref, left_ref):
        def work(at):
            right_ref[at] = a_ref[at] + b_ref[at]
            left_ref[at] = c_ref[at] + d_ref[at]

        strips(64, 8, work)

    half = pl.BlockSpec((64, HALF), lambda j: (0, 0))
    other = pl.BlockSpec((64, HALF), lambda j: (0, 1))
    extra = list(after)
    return pl.pallas_call(
        lambda *refs: kernel(*refs[:4], *refs[-2:]),
        grid=(1,),
        in_specs=[half, half, other, half] + [ANY] * len(extra),
        out_specs=[half, other],
        out_shape=[jax.ShapeDtypeStruct((64, PIECE), jnp.float32)] * 2,
        input_output_aliases={0: 0, 2: 1},
        compiler_params=pltpu.CompilerParams(vmem_limit_bytes=LIMIT),
        cost_estimate=pl.CostEstimate(flops=int(cost * 1.15e9), bytes_accessed=int(cost * 3e6), transcendentals=0),
    )(parts[1], from_left, parts[2], from_right, *extra)


def add_split(own, peer, after, cost):
    def kernel(a_ref, b_ref, *o_refs):
        for d in range(4):
            def work(at, d=d):
                from_at = pl.ds(at.start + 32 * d, at.size)
                o_refs[d][at] = a_ref[from_at] + b_ref[from_at]

            strips(32, 8, work)

    return call(
        kernel, PIECE, HALF, [(own, 0), (peer, 0)], [(32, PIECE, 0)] * 4, after, cost=cost
    )


def sum_split(terms, after, out_start, held, cost):
    def kernel(a_ref, b_ref, c_ref, *o_refs):
        for i in range(2):
            def work(at, i=i):
                from_at = pl.ds(at.start + 32 * i, at.size)
                o_refs[i][at] = a_ref[from_at] + (b_ref[from_at] + c_ref[from_at])

            strips(32, 8, work)

    return call(
        kernel, PIECE, HALF, [(t, 0) for t in terms], [(32, 2 * PIECE, out_start)] * 2, after,
        None if held is None else dict(enumerate(held)), cost=cost,
    )


def adam(terms, param, first, second, held, start, width, whole, step_start, after, cost):
    count, columns = len(terms), param.shape[1]

    def kernel(*refs):
        param_ref, first_ref, second_ref = refs[count : count + 3]
        step_ref, new_first_ref, new_second_ref = refs[-3:]

        def work(at):
            grad = refs[0][at]
            for ref in refs[1:count]:
                grad = grad + ref[at]
            new_first = 0.9 * first_ref[at] + 0.1 * grad
            new_second = 0.999 * second_ref[at] + 0.001 * grad * grad
            new_first_ref[at] = new_first
            new_second_ref[at] = new_second
            step_ref[at] = param_ref[at] - 0.1 * (new_first / (jnp.sqrt(new_second) + 1e-08))

        strips(32, 8, work)

    ins = [(t, 0) for t in terms] + [(a, start) for a in (param, first, second)]
    outs = [(32, whole, step_start), (32, columns, start), (32, columns, start)]
    return call(kernel, width, PIECE, ins, outs, after, held, cost=cost)


def mix(step, peer, held, start, columns):
    def kernel(a_ref, b_ref, o_ref):
        def work(at):
            o_ref[at] = 0.5 * a_ref[at] + 0.5 * b_ref[at]

        strips(32, 8, work)

    return call(
        kernel, step.shape[1], PIECE, [(step, 0), (peer, 0)], [(32, columns, start)], (),
        None if held is None else {0: held},
    )[0]


def to_core(value):
    return lax.ppermute(value, "fsdp", [(i, i ^ 1) for i in range(16)])


def to_y(value):
    return lax.ppermute(value, "fsdp", [(i, i ^ 8) for i in range(16)])


def to_x(value, by):
    return lax.ppermute(
        value, "fsdp", [(i, (i & 9) | ((((i >> 1) + by) & 3) << 1)) for i in range(16)]
    )


def to_rep(value, by):
    return lax.ppermute(value, "rep", [(i, (i + by) % 16) for i in range(16)])


def dealt(cot):
    me = lax.axis_index("fsdp")
    at = lax.broadcasted_iota(jnp.int32, (512, 512), 0)
    rel = lax.broadcasted_iota(jnp.int32, (512, 512), 1)
    to = rel >> 5
    core = (me ^ 1 ^ (to >> 3)) & 1
    y = ((me >> 3) ^ (to >> 2)) & 1
    x = ((me >> 1) + to) & 3
    source = (y * 8 + x * 2 + core) * 32 + (rel & 31)
    pick = (at == source).astype(cot.dtype)
    return lax.dot_general(
        pick, cot, (((0,), (1,)), ((), ())), preferred_element_type=jnp.float32
    ).astype(cot.dtype)


def push(exponent, values, work, *rest):
    def branch(power, operands):
        got = [to_rep(value, 2**power) for value in operands[0]]
        return got, work(*operands[1])

    return lax.switch(exponent, [partial(branch, p) for p in range(4)], (values, rest))


def body(param, first, second, push_weight, acts, cotangent, exponent):
    cot = dealt(cotangent[0])
    theirs, mine = cot[:256], cot[256:]
    param, first, second, acts = param[0], first[0], second[0], acts[0]
    columns = param.shape[1]
    order = (1, 3, 2)

    outs, peers, pieces = {}, {}, {}
    for i in (2, 0, 1, 3):
        before = list(outs.values())[-1:]
        acts, *before = lax.optimization_barrier((acts, *before))
        pieces[i] = acts[:, i * PIECE : (i + 1) * PIECE]
        outs[i] = product(theirs, pieces[i], 0, PIECE, before)
        peers[i] = to_core(outs[i])
    y_2 = product_add_y(mine, pieces[2], peers[2], 0, [outs[3]])
    peer_2 = to_y(y_2[1])
    x_0 = product_add_x(mine, pieces[0], peers[0], 0, y_2[:1])
    left_0, right_0 = to_x(x_0[3], 1), to_x(x_0[4], 3)
    x_1 = product_add_x(mine, pieces[1], peers[1], 0, x_0[:1])
    left_1, right_1 = to_x(x_1[3], 1), to_x(x_1[4], 3)
    both_0 = relay_add(x_0, left_0, right_0, x_1[:1], COST[0])
    in_0 = [to_x(both_0[0], 1), to_x(both_0[1], 3)]
    y_3 = product_add_y(mine, pieces[3], peers[3], 0, both_0[:1])
    peer_3 = to_y(y_3[1])
    both_1 = relay_add(x_1, left_1, right_1, y_3[:1], COST[1])
    in_1 = [to_x(both_1[0], 1), to_x(both_1[1], 3)]
    blocks_2 = add_split(y_2[0], peer_2, both_1[:1], COST[2])
    last_2 = [to_x(blocks_2[d], d) for d in order]
    halves = sum_split([x_0[0]] + in_0, blocks_2[:1], 0, None, COST[3])
    halves = sum_split([x_1[0]] + in_1, [], PIECE, halves, COST[4])
    last_0 = to_y(halves[1])
    blocks_3 = add_split(y_3[0], peer_3, halves[:1], COST[5])
    last_3 = [to_x(blocks_3[d], d) for d in order]
    moments = (param, first, second)
    step_2, *held = adam(
        [blocks_2[0]] + last_2, *moments, None, 2 * PIECE, PIECE, PIECE, 0, blocks_3[:1], COST[6]
    )
    (got_2,), _ = push(exponent[0], [step_2], lambda: ())
    step_0, *held = adam(
        [halves[0], last_0], *moments, {1: held[0], 2: held[1]}, 0, 2 * PIECE, 2 * PIECE, 0, [got_2],
        COST[7],
    )
    def finish(power, operands):
        step_0, got_0, step_1, weight, own, others, held = operands
        got_1 = to_rep(step_1, 2**power)
        got_weight = to_rep(weight, 2**power)
        step_3, *held = adam(
            [own] + others, *moments, {1: held[0], 2: held[1]}, 3 * PIECE, PIECE, PIECE, 0, [], COST[8]
        )
        got_3 = to_rep(step_3, 2**power)
        mixed = mix(step_0, got_0, None, 2 * PIECE, columns)
        mixed = mix(step_1, got_1, mixed, 0, columns)
        return mix(step_3, got_3, mixed, 3 * PIECE, columns), held, got_weight

    mixed, held, weight_peer = lax.switch(
        exponent[0],
        [partial(finish, p) for p in range(4)],
        (step_2, got_2, step_0, push_weight, blocks_3[0], last_3, held),
    )
    new_first, new_second = held
    weight = 0.5 * push_weight + 0.5 * weight_peer
    return mixed[None], new_first[None], new_second[None], weight


def solution(mesh):
    return jax.shard_map(
        body,
        mesh=mesh,
        in_specs=(
            P("rep", "fsdp", None),
            P("rep", "fsdp", None),
            P("rep", "fsdp", None),
            P("rep"),
            P("rep", "fsdp", None),
            P("rep", "fsdp", None),
            P(),
        ),
        out_specs=(
            P("rep", "fsdp", None),
            P("rep", "fsdp", None),
            P("rep", "fsdp", None),
            P("rep"),
        ),
        check_vma=False,
    )
```
